256 devices in a mesh: var: 4 (over x), tok: 2 (over z_hi), mp: 32 (over z_lo, y, core).
Axes of the slice: x: 4, y: 4, z: 8 (z_hi: 2, z_lo: 4; z = z_hi * 4 + z_lo), core: 2. Of those that a mesh axis runs over, the one named last changes fastest.
Arguments:
- patches: bfloat16 [88, 32, 64], P('var', 'tok'), may hold values from -6 to 6
- embed_weight: bfloat16 [88, 64, 12288], P('var', None, 'mp'), may hold values from -0.75 to 0.75
- embed_bias: bfloat16 [88, 12288], P('var', 'mp'), may hold values from -3 to 3
- queries: bfloat16 [32, 12288], P('tok', 'mp'), may hold values from -6 to 6
- score_bias: float32 [32, 88], P('tok'), may hold values from -4 to 260
- key_weight: bfloat16 [32, 384, 12288], P(None, 'var', 'mp'), may hold values from -0.0546875 to 0.0546875
- value_weight: bfloat16 [32, 384, 12288], P(None, 'var', 'mp'), may hold values from -0.0546875 to 0.0546875
- out_weight: bfloat16 [12288, 12288], P('mp', 'var'), may hold values from -0.109375 to 0.109375
- out_bias: bfloat16 [12288], P(('var', 'mp')), may hold values from -3 to 3
Outputs:
- aggregated: bfloat16 [32, 12288], P('tok', ('var', 'mp'))
The draws below stay inside these ranges and needn't reach their ends.
All inputs are finite; a program needn't handle non-finite values.
Results may differ from the reference program's by a relative error of at most 0.005.
Values may be sent and summed in bfloat16 or wider, within the bound.
No kernel may reach another device: no remote copies, remote signals or barrier semaphores. Data moves between devices by JAX's collectives and lax.ppermute only.
A program may use at most 128 MiB of HBM per device.

```python
import math
import jax
import jax.numpy as jnp
from jax import lax

D = 12288
HEADS = 32
HD = 384
PATCH = 64
VARS = 88
TOKENS = 32
TILES = 32
TILE = 384


def draw_score_bias(key, part):
    key = jax.random.fold_in(key, 11)
    key_base = jax.random.fold_in(key, 0)
    return jnp.clip(jax.random.normal(key_base, (TOKENS, VARS), jnp.float32), -4.0, 4.0)


def with_spikes(values, stream_key, source, target, blocks, factor):
    def block_of(axis_at):
        return (jnp.arange(values.shape[axis_at]) // (values.shape[axis_at] // blocks)).reshape((-1,) + (1,) * (values.ndim - 1 - axis_at))

    near = jax.random.permutation(stream_key, blocks)[block_of(target)]
    other_side = (block_of(target) + blocks // 2) % blocks
    return jnp.where((block_of(source) == near) | (block_of(source) == other_side), factor * values, values)


def block_levels(stream_key, dims, cuts, least, top_value):
    gain = 1.0
    for dim, parts in cuts:
        heights = jax.random.uniform(jax.random.fold_in(jax.random.fold_in(stream_key, 6), dim), (parts,), jnp.float32, least / len(cuts), top_value / len(cuts))
        gain = gain * jnp.repeat(jnp.exp(heights), dims[dim] // parts).reshape((-1,) + (1,) * (len(dims) - 1 - dim))
    return gain


def gaussian(own_key, extent, deviation, reach, shards=(), kind=jnp.bfloat16):
    values = jax.random.normal(own_key, extent, jnp.float32) * deviation
    if len(shards) > 0:
        values = block_levels(own_key, extent, shards, -0.22, 0.18) * values
    return jnp.clip(values, min=-reach, max=reach).astype(kind)


def gaussian_with(stream_key, extent, width, limit, pieces, heavy, held_as=jnp.bfloat16):
    values = width * jax.random.normal(stream_key, extent, jnp.float32)
    if pieces:
        values = values * block_levels(stream_key, extent, pieces, -0.22, 0.18)
    return jnp.clip(with_spikes(values, jax.random.fold_in(stream_key, 3), *heavy), -limit, limit).astype(held_as)


def setup_inputs(seed: int = 0) -> dict:
    key_of = jax.random.split(jax.random.key(seed), 10)
    return {
        "patches": gaussian(key_of[0], (VARS, TOKENS, PATCH), 1.0, 6.0, ((0, 4), (1, 2))),
        "embed_weight": gaussian(key_of[1], (VARS, PATCH, D), PATCH ** -0.5, 0.75, ((0, 4), (2, 32))),
        "embed_bias": gaussian(key_of[2], (VARS, D), 0.5, 3.0, ((0, 4), (1, 32))),
        "queries": gaussian(key_of[3], (TOKENS, D), 1.0, 6.0, ((0, 2), (1, 32))),
        "score_bias": draw_score_bias(jax.random.fold_in(key_of[9], 71), 0),
        "key_weight": gaussian(key_of[5], (TILES, TILE, D), D ** -0.5, 0.0546875, ((1, 4), (2, 32))),
        "value_weight": gaussian(key_of[6], (TILES, TILE, D), D ** -0.5, 0.0546875, ((1, 4), (2, 32))),
        "out_weight": gaussian_with(key_of[7], (D, D), D ** -0.5, 0.109375, ((0, 32), (1, 4)), (0, 1, 32, 2.75)),
        "out_bias": gaussian(key_of[8], (D,), 0.5, 3.0, ((0, 128),)),
    }


def reference(patches, embed_weight, embed_bias, queries, score_bias, key_weight, value_weight, out_weight, out_bias):
    embedded = jnp.einsum('vtp,vpc->vtc', patches.astype(jnp.float32), embed_weight.astype(jnp.float32), precision=lax.Precision.HIGHEST)
    embedded = (embedded + embed_bias[:, None, :].astype(jnp.float32)).astype(jnp.bfloat16)
    flat_rows = embedded.reshape(VARS * TOKENS, D)
    key_sum = jnp.dot(flat_rows, key_weight.reshape(D, D), preferred_element_type=jnp.float32)
    value_sum = jnp.dot(flat_rows, value_weight.reshape(D, D), preferred_element_type=jnp.float32)
    key_heads = key_sum.reshape(VARS, TOKENS, HEADS, HD)
    value_heads = value_sum.reshape(VARS, TOKENS, HEADS, HD)
    key_normed = key_heads * lax.rsqrt(lax.optimization_barrier(jnp.mean(key_heads * key_heads, axis=-1, keepdims=True)) + 1e-06)
    query_heads = queries.astype(jnp.float32).reshape(TOKENS, HEADS, HD)
    scores = jnp.einsum('thd,vthd->thv', query_heads, key_normed, precision=lax.Precision.HIGHEST) / math.sqrt(HD)
    scores = scores + score_bias[:, None, :]
    attention = jax.nn.softmax(scores, axis=-1)
    mixed = jnp.einsum('thv,vthd->thd', attention, value_heads, precision=lax.Precision.HIGHEST)
    mixed = mixed.astype(jnp.bfloat16).reshape(TOKENS, D)
    result = jnp.dot(mixed, out_weight, preferred_element_type=jnp.float32) + out_bias.astype(jnp.float32)[None, :]
    return result.astype(jnp.bfloat16)
```

```python
import math

import jax
import jax.numpy as jnp
from jax import lax
from jax.sharding import PartitionSpec as P

HD = 384


def on_device(
    patches,
    embed_weight,
    embed_bias,
    queries,
    score_bias,
    key_weight,
    value_weight,
    out_weight,
    out_bias,
):
    var_count = lax.axis_size("var")
    mp_count = lax.axis_size("mp")
    var_place = lax.axis_index("var")
    local_vars, tok_rows, _ = patches.shape
    all_vars = local_vars * var_count
    tile_width = embed_weight.shape[2]
    quarter = tile_width // var_count
    part_tokens = tok_rows // var_count
    embedded = jnp.einsum("vpc,vtp->vct", embed_weight, patches, preferred_element_type=jnp.float32)
    embedded = (embedded + embed_bias[:, :, None].astype(jnp.float32)).astype(jnp.bfloat16)
    own = embedded.transpose(1, 2, 0).reshape(var_count, quarter, tok_rows, local_vars)
    received = lax.all_to_all(own, "var", split_axis=0, concat_axis=3, tiled=True)
    block = received.reshape(quarter, tok_rows * all_vars)
    gathered = lax.all_gather(block, "mp", axis=0, tiled=True)
    features = mp_count * quarter
    key_part = lax.dot_general(
        key_weight.reshape(features, tile_width), gathered, (((0,), (0,)), ((), ())),
        preferred_element_type=jnp.float32,
    ).astype(jnp.bfloat16)
    value_part = lax.dot_general(
        value_weight.reshape(features, tile_width), gathered, (((0,), (0,)), ((), ())),
        preferred_element_type=jnp.float32,
    ).astype(jnp.bfloat16)
    parts = jnp.stack([key_part, value_part]).reshape(
        2, tile_width, var_count, part_tokens * all_vars
    ).transpose(2, 0, 1, 3)
    parts = lax.all_to_all(parts, "var", split_axis=0, concat_axis=0, tiled=True)
    totals = parts.astype(jnp.float32).sum(0)
    heads_here = tile_width // HD
    totals = totals.reshape(2, heads_here, HD, part_tokens, all_vars)
    keys, values = totals[0], totals[1]
    scale = lax.rsqrt(jnp.mean(keys * keys, axis=1) + 1e-06)
    query_rows = lax.dynamic_slice_in_dim(queries, var_place * part_tokens, part_tokens, 0)
    query_heads = query_rows.astype(jnp.float32).reshape(part_tokens, heads_here, HD).transpose(1, 2, 0)
    bias_rows = lax.dynamic_slice_in_dim(score_bias, var_place * part_tokens, part_tokens, 0)
    scores = (query_heads[..., None] * keys).sum(1) * scale / math.sqrt(HD)
    attention = jax.nn.softmax(scores + bias_rows[None], axis=-1)
    mixed = (attention[:, None] * values).sum(-1).transpose(2, 0, 1)
    mixed = mixed.astype(jnp.bfloat16).reshape(part_tokens, tile_width)
    every_token = lax.all_gather(mixed, "var", axis=0, tiled=True)
    product = jnp.dot(every_token, out_weight, preferred_element_type=jnp.float32)
    product = product.astype(jnp.bfloat16).reshape(tok_rows, mp_count, -1).transpose(1, 0, 2)
    terms = lax.all_to_all(product, "mp", split_axis=0, concat_axis=0, tiled=True)
    summed = terms.astype(jnp.float32).sum(0)
    return (summed + out_bias.astype(jnp.float32)[None, :]).astype(jnp.bfloat16)


def solution(mesh):
    in_specs = (
        P("var", "tok", None),
        P("var", None, "mp"),
        P("var", "mp"),
        P("tok", "mp"),
        P("tok", None),
        P(None, "var", "mp"),
        P(None, "var", "mp"),
        P("mp", "var"),
        P(("var", "mp")),
    )
    out_specs = P("tok", ("var", "mp"))
    return jax.shard_map(
        on_device, mesh=mesh, in_specs=in_specs, out_specs=out_specs, check_vma=False
    )
```

```python
import functools
import math

import jax
import jax.numpy as jnp
import numpy as np
from jax import lax
from jax.experimental import pallas as pl
from jax.experimental.pallas import tpu as pltpu
from jax.sharding import PartitionSpec as P

HD = 384
Z, Y, C = 4, 4, 2
STEPS = (2, 1, 3, 0)
COST = 2**16
VMEM = 8 * 2**20


def move(array, there):
    pairs = []
    for z in range(Z):
        for y in range(Y):
            for c in range(C):
                z2, y2, c2 = there(z, y, c)
                pairs.append(((z * Y + y) * C + c, ((z2 % Z) * Y + y2 % Y) * C + c2 % C))
    return lax.ppermute(array, "mp", pairs)


def other_core(array):
    return move(array, lambda z, y, c: (z, y, 1 - c))


def along_z(array, step):
    return move(array, lambda z, y, c: (z + step, y, c))


def along_y(array):
    return move(array, lambda z, y, c: (z, y + 1 - 2 * c, c))


def local_call(kernel, after, arrays, specs, out_shape, out_block, name, aliases=None):
    return pl.pallas_call(
        kernel,
        grid=(1,),
        in_specs=[pl.BlockSpec(memory_space=pl.ANY)] + specs,
        out_specs=out_block,
        out_shape=jax.ShapeDtypeStruct(out_shape, jnp.bfloat16),
        input_output_aliases=aliases or {},
        compiler_params=pltpu.CompilerParams(vmem_limit_bytes=VMEM),
        cost_estimate=pl.CostEstimate(flops=0, transcendentals=0, bytes_accessed=COST),
        name=name,
    )(after, *arrays)


def copy_kernel(after, array, out):
    out[...] = array[...]


def pack_kernel(after, received, out):
    owners, groups, _, width = received.shape
    for group in range(groups):
        for owner in range(owners):
            out[group, :, owner * width : (owner + 1) * width] = received[owner, group]


def pack(received, after):
    owners, groups, rows, width = received.shape
    shape = (groups, rows, owners * width)
    return local_call(
        pack_kernel,
        after,
        [received],
        [pl.BlockSpec(received.shape, lambda k: (0, 0, 0, 0))],
        shape,
        pl.BlockSpec(shape, lambda k: (0, 0, 0)),
        "pack",
    )


def first_half(array, after):
    rows, width = array.shape
    block = pl.BlockSpec((rows, width // 2), lambda k: (0, 0))
    return local_call(copy_kernel, after, [array], [block], (rows, width // 2), block, "half")


def line_kernel(chunk, groups, after, *refs):
    *parts, out, wide = refs
    tile = out.shape[1] // len(parts)
    rows = parts[0].shape[1]
    for n, part in enumerate(parts):
        values = part[groups[chunk]].astype(jnp.float32)
        for block in range(values.shape[1] // tile):
            wide[block * rows : (block + 1) * rows, n * tile : (n + 1) * tile] = values[
                :, block * tile : (block + 1) * tile
            ]
    out[...] = wide[...].astype(out.dtype)


def line_of(parts, chunk, groups, after):
    _, rows, width = parts[0].shape
    tile = width // 4
    shape = (rows * 4, tile * len(parts))
    return pl.pallas_call(
        functools.partial(line_kernel, chunk),
        in_specs=[pl.BlockSpec(memory_space=pltpu.SMEM), pl.BlockSpec(memory_space=pl.ANY)]
        + [pl.BlockSpec(memory_space=pltpu.VMEM) for _ in parts],
        out_specs=pl.BlockSpec(memory_space=pltpu.VMEM),
        out_shape=jax.ShapeDtypeStruct(shape, jnp.bfloat16),
        scratch_shapes=[pltpu.VMEM(shape, jnp.float32)],
        compiler_params=pltpu.CompilerParams(vmem_limit_bytes=VMEM),
        cost_estimate=pl.CostEstimate(flops=0, transcendentals=0, bytes_accessed=COST),
        name="line",
    )(groups, after, *parts)


def order_kernel(order, keys, values, *refs):
    count = len(refs) - 3
    outs, (held, sems, out_sems) = refs[:count], refs[count:]
    width = keys.shape[2]
    copies, leaving = [], []
    for n in range(keys.shape[0]):
        for k, weight in enumerate((keys, values)):
            copy = pltpu.make_async_copy(
                weight.at[order[n]], held.at[n, :, pl.ds(k * width, width)], sems.at[k, n]
            )
            copy.start()
            copies.append(copy)
    first = 0
    for m, out in enumerate(outs):
        last = first + out.shape[0]
        for copy in copies[2 * first : 2 * last]:
            copy.wait()
        leaving.append(
            pltpu.make_async_copy(held.at[pl.ds(first, last - first)], out, out_sems.at[m])
        )
        leaving[-1].start()
        first = last
    for copy in leaving:
        copy.wait()


def ordered_weights(order, keys, values, counts):
    tiles, rows, width = keys.shape
    anywhere = pl.BlockSpec(memory_space=pl.ANY)
    return pl.pallas_call(
        order_kernel,
        in_specs=[pl.BlockSpec(memory_space=pltpu.SMEM), anywhere, anywhere],
        out_specs=[pl.BlockSpec(memory_space=pltpu.HBM) for _ in counts],
        out_shape=[pltpu.HBM((n, rows, 2 * width), keys.dtype) for n in counts],
        scratch_shapes=[
            pltpu.VMEM((tiles, rows, 2 * width), keys.dtype),
            pltpu.SemaphoreType.DMA((2, tiles)),
            pltpu.SemaphoreType.DMA((len(counts),)),
        ],
        compiler_params=pltpu.CompilerParams(vmem_limit_bytes=VMEM),
        cost_estimate=pl.CostEstimate(flops=0, transcendentals=0, bytes_accessed=10 * 2**20),
        name="order_weights",
    )(order, keys, values)


def arrival_order(ids):
    def sent(ids, there):
        result = np.zeros_like(ids)
        for n in range(Z * Y * C):
            z, y, c = there(n // (Y * C), n // C % Y, n % C)
            result[(z % Z * Y + y % Y) * C + c % C] = ids[n]
        return result

    def up_or_down(ids):
        return sent(ids, lambda z, y, c: (z, y + 1 - 2 * c, c))

    def swapped(ids):
        return sent(ids, lambda z, y, c: (z, y, 1 - c))

    mine = [ids] + [sent(ids, lambda z, y, c: (z + step, y, c)) for step in (1, 3, 2)]
    line = np.concatenate(mine + [swapped(part) for part in mine], axis=1)
    near = up_or_down(line)
    far = up_or_down(near[:, : near.shape[1] // 2])
    return np.concatenate([line, near, swapped(near), far, swapped(far)], axis=1)


def core_var_shift(array):
    n = lax.axis_size("var")
    m = lax.axis_size("mp")
    pairs = [
        (k * m + p, (k + 1 - 2 * (p % C)) % n * m + p) for k in range(n) for p in range(m)
    ]
    return lax.ppermute(array, ("var", "mp"), pairs)


def var_shift(array, step):
    n = lax.axis_size("var")
    return lax.ppermute(array, "var", [(k, (k + step) % n) for k in range(n)])


def on_device(
    patches,
    embed_weight,
    embed_bias,
    queries,
    score_bias,
    key_weight,
    value_weight,
    out_weight,
    out_bias,
):
    var_count = lax.axis_size("var")
    mp_count = lax.axis_size("mp")
    var_place = lax.axis_index("var")
    local_vars, tok_rows, _ = patches.shape
    all_vars = local_vars * var_count
    tile_width = embed_weight.shape[2]
    quarter = tile_width // var_count
    part_tokens = tok_rows // var_count
    rows = part_tokens * all_vars
    f32 = jnp.float32
    embedded = jnp.einsum("vtp,vpc->vtc", patches, embed_weight, preferred_element_type=f32)
    embedded = (embedded + embed_bias[:, None, :].astype(f32)).astype(jnp.bfloat16)
    own = embedded.reshape(local_vars, var_count, part_tokens, var_count, quarter)
    own = own.transpose(3, 1, 0, 2, 4).reshape(var_count, var_count, -1, quarter)
    order = arrival_order(np.arange(mp_count)[:, None])
    order = jnp.take(jnp.asarray(order, jnp.int32), lax.axis_index("mp"), axis=0)
    weights = ordered_weights(order, key_weight, value_weight, (8, 8, 8, 4, 4))
    received = lax.all_to_all(own, "var", split_axis=0, concat_axis=0, tiled=True)
    tiles = pack(received, weights[0])
    weights = [w.reshape(-1, 2 * tile_width) for w in weights]
    tiles = [tiles] + [along_z(tiles, step) for step in (1, 3, 2)]
    tiles += [other_core(part) for part in tiles]
    groups = jnp.stack([(var_place + step) % var_count for step in STEPS]).astype(jnp.int32)

    def line(chunk, after):
        return line_of(tiles, chunk, groups, after)

    def product(line, near, half):
        far = along_y(half)
        parts = [line, near, other_core(near), far, other_core(far)]
        total = 0.0
        for part, weight in zip(parts, weights):
            total = total + jnp.dot(part, weight, preferred_element_type=f32)
        return total

    core = lax.axis_index("mp") % C
    line0 = line(0, out_bias)
    near0 = along_y(line0)
    line1 = line(1, line0)
    near1 = along_y(line1)
    half0 = first_half(near0, line1)
    line2 = line(2, half0)
    near2 = along_y(line2)
    line3 = line(3, line2)
    near3 = along_y(line3)
    far_sent = product(line0, near0, half0).astype(jnp.bfloat16)
    far = core_var_shift(far_sent).astype(f32)
    half1 = first_half(near1, far_sent)
    half2 = first_half(near2, half1)
    ahead = product(line1, near1, half1)
    ahead_sent = (ahead + jnp.where(core == 0, far, 0.0)).astype(jnp.bfloat16)
    half3 = first_half(near3, ahead_sent)
    behind = product(line2, near2, half2)
    from_behind = var_shift(ahead_sent, 1)
    from_ahead = var_shift((behind + jnp.where(core == 1, far, 0.0)).astype(jnp.bfloat16), -1)
    totals = product(line3, near3, half3)
    totals = totals + from_behind.astype(f32) + from_ahead.astype(f32)

    keys, values = totals[:, :tile_width], totals[:, tile_width:]
    scale = lax.rsqrt(jnp.mean(keys * keys, axis=1) + 1e-06)
    query_rows = lax.dynamic_slice_in_dim(queries, var_place * part_tokens, part_tokens, 0)
    bias_rows = lax.dynamic_slice_in_dim(score_bias, var_place * part_tokens, part_tokens, 0)
    token = np.arange(rows) % part_tokens
    spot = jnp.asarray(token[:, None] == np.arange(part_tokens))
    spread = jnp.dot(spot.astype(jnp.bfloat16), query_rows, preferred_element_type=f32)
    scores = (spread * keys).sum(1) * scale / math.sqrt(HD) + bias_rows.T.reshape(rows)
    scores = jnp.where(spot, scores[:, None], -jnp.inf)
    weight = jnp.exp(scores - scores.max(0, keepdims=True))
    attention = weight / weight.sum(0, keepdims=True)
    mixed = lax.dot_general(
        attention, values, (((0,), (0,)), ((), ())), precision=lax.Precision.HIGHEST
    ).astype(jnp.bfloat16)

    every_token = jnp.zeros((tok_rows, tile_width), jnp.bfloat16)
    for step in range(var_count):
        piece = var_shift(mixed, step) if step else mixed
        place = (var_place - step) % var_count
        every_token = lax.dynamic_update_slice_in_dim(every_token, piece, place * part_tokens, 0)
    product = jnp.dot(every_token, out_weight, preferred_element_type=f32)
    product = product.astype(jnp.bfloat16).reshape(tok_rows, mp_count, -1).transpose(1, 0, 2)
    terms = lax.all_to_all(product, "mp", split_axis=0, concat_axis=0, tiled=True)
    summed = terms.astype(f32).sum(0)
    return (summed + out_bias.astype(f32)[None, :]).astype(jnp.bfloat16)


def solution(mesh):
    in_specs = (
        P("var", "tok", None),
        P("var", None, "mp"),
        P("var", "mp"),
        P("tok", "mp"),
        P("tok", None),
        P(None, "var", "mp"),
        P(None, "var", "mp"),
        P("mp", "var"),
        P(("var", "mp")),
    )
    out_specs = P("tok", ("var", "mp"))
    return jax.shard_map(
        on_device, mesh=mesh, in_specs=in_specs, out_specs=out_specs, check_vma=False
    )
```

```python
import functools
import math

import jax
import jax.numpy as jnp
import numpy as np
from jax import lax
from jax.experimental import pallas as pl
from jax.experimental.pallas import tpu as pltpu
from jax.sharding import PartitionSpec as P

HD = 384
Z, Y, C = 4, 4, 2
STEPS = (2, 1, 3, 0)
COST = 2**16
VMEM = 8 * 2**20


def move(array, there):
    pairs = []
    for z in range(Z):
        for y in range(Y):
            for c in range(C):
                z2, y2, c2 = there(z, y, c)
                pairs.append(((z * Y + y) * C + c, ((z2 % Z) * Y + y2 % Y) * C + c2 % C))
    return lax.ppermute(array, "mp", pairs)


def other_core(array):
    return move(array, lambda z, y, c: (z, y, 1 - c))


def along_z(array, step):
    return move(array, lambda z, y, c: (z + step, y, c))


def along_y(array):
    return move(array, lambda z, y, c: (z, y + 1 - 2 * c, c))


def local_call(
    kernel, after, arrays, specs, out_shape, out_block, name, dtype=jnp.bfloat16
):
    return pl.pallas_call(
        kernel,
        grid=(1,),
        in_specs=[pl.BlockSpec(memory_space=pl.ANY)] + specs,
        out_specs=out_block,
        out_shape=jax.ShapeDtypeStruct(out_shape, dtype),
        compiler_params=pltpu.CompilerParams(vmem_limit_bytes=VMEM),
        cost_estimate=pl.CostEstimate(flops=0, transcendentals=0, bytes_accessed=COST),
        name=name,
    )(after, *arrays)


def copy_kernel(after, array, out):
    out[...] = array[...]


def pack_kernel(first, groups, after, received, out):
    owners, width = received.shape[0], received.shape[3]
    for chunk in range(out.shape[0]):
        for owner in range(owners):
            out[chunk, :, owner * width : (owner + 1) * width] = received[
                owner, groups[first + chunk]
            ]


def pack(received, groups, first, count, after):
    owners, _, rows, width = received.shape
    return pl.pallas_call(
        functools.partial(pack_kernel, first),
        in_specs=[
            pl.BlockSpec(memory_space=pltpu.SMEM),
            pl.BlockSpec(memory_space=pl.ANY),
            pl.BlockSpec(memory_space=pltpu.VMEM),
        ],
        out_specs=pl.BlockSpec(memory_space=pltpu.VMEM),
        out_shape=jax.ShapeDtypeStruct((count, rows, owners * width), jnp.bfloat16),
        compiler_params=pltpu.CompilerParams(vmem_limit_bytes=VMEM),
        cost_estimate=pl.CostEstimate(flops=0, transcendentals=0, bytes_accessed=COST),
        name="pack",
    )(groups, after, received)


def first_half(array, after):
    rows, width = array.shape
    block = pl.BlockSpec((rows, width // 2), lambda k: (0, 0))
    return local_call(copy_kernel, after, [array], [block], (rows, width // 2), block, "half")


def line_kernel(chunk, first, second, *refs):
    *parts, out, wide = refs
    tile = out.shape[1] // len(parts)
    rows = parts[0].shape[1]
    for n, part in enumerate(parts):
        values = part[chunk].astype(jnp.float32)
        for block in range(values.shape[1] // tile):
            wide[block * rows : (block + 1) * rows, n * tile : (n + 1) * tile] = values[
                :, block * tile : (block + 1) * tile
            ]
    out[...] = wide[...].astype(out.dtype)


def line_of(parts, chunk, *after):
    _, rows, width = parts[0].shape
    tile = width // 4
    shape = (rows * 4, tile * len(parts))
    return pl.pallas_call(
        functools.partial(line_kernel, chunk),
        in_specs=[pl.BlockSpec(memory_space=pl.ANY)] * 2
        + [pl.BlockSpec(memory_space=pltpu.VMEM) for _ in parts],
        out_specs=pl.BlockSpec(memory_space=pltpu.VMEM),
        out_shape=jax.ShapeDtypeStruct(shape, jnp.bfloat16),
        scratch_shapes=[pltpu.VMEM(shape, jnp.float32)],
        compiler_params=pltpu.CompilerParams(vmem_limit_bytes=VMEM),
        cost_estimate=pl.CostEstimate(flops=0, transcendentals=0, bytes_accessed=COST),
        name="line",
    )(*after, *parts)


def copied(array, after):
    block = pl.BlockSpec(array.shape, lambda k: (0,) * array.ndim)
    return local_call(
        copy_kernel, after, [array], [block], array.shape, block, "copied", array.dtype
    )


def order_kernel(order, keys, values, *refs):
    *outs, done, held, sems, out_sems = refs
    done[...] = jnp.zeros_like(done)
    width = keys.shape[2]
    copies, leaving = [], []
    for n in range(keys.shape[0]):
        for k, weight in enumerate((keys, values)):
            copy = pltpu.make_async_copy(
                weight.at[order[n]], held.at[n, :, pl.ds(k * width, width)], sems.at[k, n]
            )
            copy.start()
            copies.append(copy)
    first = 0
    for m, out in enumerate(outs):
        last = first + out.shape[0]
        for copy in copies[2 * first : 2 * last]:
            copy.wait()
        leaving.append(
            pltpu.make_async_copy(held.at[pl.ds(first, last - first)], out, out_sems.at[m])
        )
        leaving[-1].start()
        first = last
    for copy in leaving:
        copy.wait()


def ordered_weights(order, keys, values, counts):
    tiles, rows, width = keys.shape
    anywhere = pl.BlockSpec(memory_space=pl.ANY)
    return pl.pallas_call(
        order_kernel,
        in_specs=[pl.BlockSpec(memory_space=pltpu.SMEM), anywhere, anywhere],
        out_specs=[pl.BlockSpec(memory_space=pltpu.HBM) for _ in counts]
        + [pl.BlockSpec(memory_space=pltpu.VMEM)],
        out_shape=[pltpu.HBM((n, rows, 2 * width), keys.dtype) for n in counts]
        + [jax.ShapeDtypeStruct((8, 128), jnp.float32)],
        scratch_shapes=[
            pltpu.VMEM((tiles, rows, 2 * width), keys.dtype),
            pltpu.SemaphoreType.DMA((2, tiles)),
            pltpu.SemaphoreType.DMA((len(counts),)),
        ],
        compiler_params=pltpu.CompilerParams(vmem_limit_bytes=VMEM),
        cost_estimate=pl.CostEstimate(flops=0, transcendentals=0, bytes_accessed=10 * 2**20),
        name="order_weights",
    )(order, keys, values)


def arrival_order(ids):
    def sent(ids, there):
        result = np.zeros_like(ids)
        for n in range(Z * Y * C):
            z, y, c = there(n // (Y * C), n // C % Y, n % C)
            result[(z % Z * Y + y % Y) * C + c % C] = ids[n]
        return result

    def up_or_down(ids):
        return sent(ids, lambda z, y, c: (z, y + 1 - 2 * c, c))

    def swapped(ids):
        return sent(ids, lambda z, y, c: (z, y, 1 - c))

    mine = [ids] + [sent(ids, lambda z, y, c: (z + step, y, c)) for step in (1, 3, 2)]
    line = np.concatenate(mine + [swapped(part) for part in mine], axis=1)
    near = up_or_down(line)
    far = up_or_down(near[:, : near.shape[1] // 2])
    return np.concatenate([line, near, swapped(near), far, swapped(far)], axis=1)


def core_var_shift(array):
    n = lax.axis_size("var")
    m = lax.axis_size("mp")
    pairs = [
        (k * m + p, (k + 1 - 2 * (p % C)) % n * m + p) for k in range(n) for p in range(m)
    ]
    return lax.ppermute(array, ("var", "mp"), pairs)


def var_shift(array, step):
    n = lax.axis_size("var")
    return lax.ppermute(array, "var", [(k, (k + step) % n) for k in range(n)])


def on_device(
    patches,
    embed_weight,
    embed_bias,
    queries,
    score_bias,
    key_weight,
    value_weight,
    out_weight,
    out_bias,
):
    var_count = lax.axis_size("var")
    mp_count = lax.axis_size("mp")
    var_place = lax.axis_index("var")
    local_vars, tok_rows, _ = patches.shape
    all_vars = local_vars * var_count
    tile_width = embed_weight.shape[2]
    quarter = tile_width // var_count
    part_tokens = tok_rows // var_count
    rows = part_tokens * all_vars
    f32 = jnp.float32
    embedded = jnp.einsum("vtp,vpc->vtc", patches, embed_weight, preferred_element_type=f32)
    embedded = (embedded + embed_bias[:, None, :].astype(f32)).astype(jnp.bfloat16)
    own = embedded.reshape(local_vars, var_count, part_tokens, var_count, quarter)
    own = own.transpose(3, 1, 0, 2, 4).reshape(var_count, var_count, -1, quarter)
    order = arrival_order(np.arange(mp_count)[:, None])
    order = jnp.take(jnp.asarray(order, jnp.int32), lax.axis_index("mp"), axis=0)
    *weights, ordered = ordered_weights(order, key_weight, value_weight, (8, 8, 8, 4, 4))
    received = lax.all_to_all(own, "var", split_axis=0, concat_axis=0, tiled=True)
    groups = jnp.stack([(var_place + step) % var_count for step in STEPS]).astype(jnp.int32)
    weights = [w.reshape(-1, 2 * tile_width) for w in weights]
    early = pack(received, groups, 0, 2, ordered)
    late = pack(received, groups, 2, 2, early)
    early = [early] + [along_z(early, step) for step in (1, 3, 2)]
    late = [late] + [along_z(late, step) for step in (1, 3, 2)]
    early += [other_core(part) for part in early]

    def product(line, near, far):
        total = 0.0
        for part, weight in zip([line, near, other_core(near), far, other_core(far)], weights):
            total = total + jnp.dot(part, weight, preferred_element_type=f32)
        return total

    core = lax.axis_index("mp") % C
    line0 = line_of(early, 0, late[1], late[2])
    near0 = along_y(line0)
    line1 = line_of(early, 1, line0, line0)
    near1 = along_y(line1)
    half0 = first_half(near0, line1)
    far0 = along_y(half0)
    late[3] = copied(late[3], half0)
    late += [other_core(part) for part in late]
    half1 = first_half(near1, half0)
    far1 = along_y(half1)
    line2 = line_of(late, 0, half1, half1)
    near2 = along_y(line2)
    far0 = copied(far0, line2)
    far_sent = product(line0, near0, far0).astype(jnp.bfloat16)
    far = core_var_shift(far_sent).astype(f32)
    half2 = first_half(near2, far_sent)
    far2 = along_y(half2)
    line3 = line_of(late, 1, half2, half2)
    near3 = along_y(line3)
    far1 = copied(far1, line3)
    ahead_sent = product(line1, near1, far1) + jnp.where(core == 0, far, 0.0)
    ahead_sent = ahead_sent.astype(jnp.bfloat16)
    far2 = copied(far2, far1)
    behind_sent = product(line2, near2, far2) + jnp.where(core == 1, far, 0.0)
    behind_sent = behind_sent.astype(jnp.bfloat16)
    from_behind = var_shift(ahead_sent, 1)
    from_ahead = var_shift(behind_sent, -1)
    half3 = first_half(near3, behind_sent)
    far3 = along_y(half3)
    totals = product(line3, near3, far3)
    totals = totals + from_behind.astype(f32) + from_ahead.astype(f32)

    keys, values = totals[:, :tile_width], totals[:, tile_width:]
    scale = lax.rsqrt(jnp.mean(keys * keys, axis=1) + 1e-06)
    query_rows = lax.dynamic_slice_in_dim(
        copied(queries, behind_sent), var_place * part_tokens, part_tokens, 0)
    bias_rows = lax.dynamic_slice_in_dim(
        copied(score_bias, behind_sent), var_place * part_tokens, part_tokens, 0)
    token = np.arange(rows) % part_tokens
    spot = jnp.asarray(token[:, None] == np.arange(part_tokens))
    spread = jnp.dot(spot.astype(jnp.bfloat16), query_rows, preferred_element_type=f32)
    spread = lax.optimization_barrier(spread)
    scores = (spread * keys).sum(1) * scale / math.sqrt(HD) + bias_rows.T.reshape(rows)
    scores = jnp.where(spot, scores[:, None], -jnp.inf)
    weight = jnp.exp(scores - scores.max(0, keepdims=True))
    attention = weight / weight.sum(0, keepdims=True)
    mixed = lax.dot_general(
        attention, values, (((0,), (0,)), ((), ())), precision=lax.Precision.HIGHEST
    ).astype(jnp.bfloat16)

    every_token = jnp.zeros((tok_rows, tile_width), jnp.bfloat16)
    for step in (2, 1, 3, 0):
        piece = var_shift(mixed, step) if step else mixed
        place = (var_place - step) % var_count
        every_token = lax.dynamic_update_slice_in_dim(every_token, piece, place * part_tokens, 0)
    product = jnp.dot(every_token, out_weight, preferred_element_type=f32)
    product = product.astype(jnp.bfloat16).reshape(tok_rows, mp_count, -1).transpose(1, 0, 2)
    terms = lax.all_to_all(product, "mp", split_axis=0, concat_axis=0, tiled=True)
    summed = terms.astype(f32).sum(0)
    return (summed + out_bias.astype(f32)[None, :]).astype(jnp.bfloat16)


def solution(mesh):
    in_specs = (
        P("var", "tok", None),
        P("var", None, "mp"),
        P("var", "mp"),
        P("tok", "mp"),
        P("tok", None),
        P(None, "var", "mp"),
        P(None, "var", "mp"),
        P("mp", "var"),
        P(("var", "mp")),
    )
    out_specs = P("tok", ("var", "mp"))
    return jax.shard_map(
        on_device, mesh=mesh, in_specs=in_specs, out_specs=out_specs, check_vma=False
    )
```

```python
import functools
import math

import jax
import jax.numpy as jnp
import numpy as np
from jax import lax
from jax.experimental import pallas as pl
from jax.experimental.pallas import tpu as pltpu
from jax.sharding import PartitionSpec as P

HD = 384
Z, Y, C = 4, 4, 2
STEPS = (2, 1, 3, 0)
COST = 2**16
VMEM = 8 * 2**20


def move(array, there):
    pairs = []
    for z in range(Z):
        for y in range(Y):
            for c in range(C):
                z2, y2, c2 = there(z, y, c)
                pairs.append(((z * Y + y) * C + c, ((z2 % Z) * Y + y2 % Y) * C + c2 % C))
    return lax.ppermute(array, "mp", pairs)


def other_core(array):
    return move(array, lambda z, y, c: (z, y, 1 - c))


def along_z(array, step):
    return move(array, lambda z, y, c: (z + step, y, c))


def along_y(array):
    return move(array, lambda z, y, c: (z, y + 1 - 2 * c, c))


def local_call(kernel, after, arrays, specs, out_shape, out_block, name, aliases=None):
    return pl.pallas_call(
        kernel,
        grid=(1,),
        in_specs=[pl.BlockSpec(memory_space=pl.ANY)] + specs,
        out_specs=out_block,
        out_shape=jax.ShapeDtypeStruct(out_shape, jnp.bfloat16),
        input_output_aliases=aliases or {},
        compiler_params=pltpu.CompilerParams(vmem_limit_bytes=VMEM),
        cost_estimate=pl.CostEstimate(flops=0, transcendentals=0, bytes_accessed=COST),
        name=name,
    )(after, *arrays)


def copy_kernel(after, array, out):
    out[...] = array[...]


def pack_kernel(first, groups, after, received, out):
    owners, width = received.shape[0], received.shape[3]
    for chunk in range(out.shape[0]):
        for owner in range(owners):
            out[chunk, :, owner * width : (owner + 1) * width] = received[
                owner, groups[first + chunk]
            ]


def pack(received, groups, first, count, after):
    owners, _, rows, width = received.shape
    return pl.pallas_call(
        functools.partial(pack_kernel, first),
        in_specs=[
            pl.BlockSpec(memory_space=pltpu.SMEM),
            pl.BlockSpec(memory_space=pl.ANY),
            pl.BlockSpec(memory_space=pltpu.VMEM),
        ],
        out_specs=pl.BlockSpec(memory_space=pltpu.VMEM),
        out_shape=jax.ShapeDtypeStruct((count, rows, owners * width), jnp.bfloat16),
        compiler_params=pltpu.CompilerParams(vmem_limit_bytes=VMEM),
        cost_estimate=pl.CostEstimate(flops=0, transcendentals=0, bytes_accessed=COST),
        name="pack",
    )(groups, after, received)


def first_half(array, after):
    rows, width = array.shape
    block = pl.BlockSpec((rows, width // 2), lambda k: (0, 0))
    return local_call(copy_kernel, after, [array], [block], (rows, width // 2), block, "half")


def line_kernel(chunk, first, second, *refs):
    *parts, out, wide = refs
    tile = out.shape[1] // len(parts)
    rows = parts[0].shape[1]
    for n, part in enumerate(parts):
        values = part[chunk].astype(jnp.float32)
        for block in range(values.shape[1] // tile):
            wide[block * rows : (block + 1) * rows, n * tile : (n + 1) * tile] = values[
                :, block * tile : (block + 1) * tile
            ]
    out[...] = wide[...].astype(out.dtype)


def line_of(parts, chunk, *after):
    _, rows, width = parts[0].shape
    tile = width // 4
    shape = (rows * 4, tile * len(parts))
    return pl.pallas_call(
        functools.partial(line_kernel, chunk),
        in_specs=[pl.BlockSpec(memory_space=pl.ANY)] * 2
        + [pl.BlockSpec(memory_space=pltpu.VMEM) for _ in parts],
        out_specs=pl.BlockSpec(memory_space=pltpu.VMEM),
        out_shape=jax.ShapeDtypeStruct(shape, jnp.bfloat16),
        scratch_shapes=[pltpu.VMEM(shape, jnp.float32)],
        compiler_params=pltpu.CompilerParams(vmem_limit_bytes=VMEM),
        cost_estimate=pl.CostEstimate(flops=0, transcendentals=0, bytes_accessed=COST),
        name="line",
    )(*after, *parts)


def copied(array, after):
    block = pl.BlockSpec(array.shape, lambda k: (0, 0))
    return local_call(copy_kernel, after, [array], [block], array.shape, block, "copied")


def order_kernel(order, keys, values, *refs):
    *outs, done, held, sems, out_sems = refs
    done[...] = jnp.zeros_like(done)
    width = keys.shape[2]
    copies, leaving = [], []
    for n in range(keys.shape[0]):
        for k, weight in enumerate((keys, values)):
            copy = pltpu.make_async_copy(
                weight.at[order[n]], held.at[n, :, pl.ds(k * width, width)], sems.at[k, n]
            )
            copy.start()
            copies.append(copy)
    first = 0
    for m, out in enumerate(outs):
        last = first + out.shape[0]
        for copy in copies[2 * first : 2 * last]:
            copy.wait()
        leaving.append(
            pltpu.make_async_copy(held.at[pl.ds(first, last - first)], out, out_sems.at[m])
        )
        leaving[-1].start()
        first = last
    for copy in leaving:
        copy.wait()


def ordered_weights(order, keys, values, counts):
    tiles, rows, width = keys.shape
    anywhere = pl.BlockSpec(memory_space=pl.ANY)
    return pl.pallas_call(
        order_kernel,
        in_specs=[pl.BlockSpec(memory_space=pltpu.SMEM), anywhere, anywhere],
        out_specs=[pl.BlockSpec(memory_space=pltpu.HBM) for _ in counts]
        + [pl.BlockSpec(memory_space=pltpu.VMEM)],
        out_shape=[pltpu.HBM((n, rows, 2 * width), keys.dtype) for n in counts]
        + [jax.ShapeDtypeStruct((8, 128), jnp.float32)],
        scratch_shapes=[
            pltpu.VMEM((tiles, rows, 2 * width), keys.dtype),
            pltpu.SemaphoreType.DMA((2, tiles)),
            pltpu.SemaphoreType.DMA((len(counts),)),
        ],
        compiler_params=pltpu.CompilerParams(vmem_limit_bytes=VMEM),
        cost_estimate=pl.CostEstimate(flops=0, transcendentals=0, bytes_accessed=10 * 2**20),
        name="order_weights",
    )(order, keys, values)


def arrival_order(ids):
    def sent(ids, there):
        result = np.zeros_like(ids)
        for n in range(Z * Y * C):
            z, y, c = there(n // (Y * C), n // C % Y, n % C)
            result[(z % Z * Y + y % Y) * C + c % C] = ids[n]
        return result

    def up_or_down(ids):
        return sent(ids, lambda z, y, c: (z, y + 1 - 2 * c, c))

    def swapped(ids):
        return sent(ids, lambda z, y, c: (z, y, 1 - c))

    mine = [ids] + [sent(ids, lambda z, y, c: (z + step, y, c)) for step in (1, 3, 2)]
    line = np.concatenate(mine + [swapped(part) for part in mine], axis=1)
    near = up_or_down(line)
    far = up_or_down(near[:, : near.shape[1] // 2])
    return np.concatenate([line, near, swapped(near), far, swapped(far)], axis=1)


def core_var_shift(array):
    n = lax.axis_size("var")
    m = lax.axis_size("mp")
    pairs = [
        (k * m + p, (k + 1 - 2 * (p % C)) % n * m + p) for k in range(n) for p in range(m)
    ]
    return lax.ppermute(array, ("var", "mp"), pairs)


def var_shift(array, step):
    n = lax.axis_size("var")
    return lax.ppermute(array, "var", [(k, (k + step) % n) for k in range(n)])


def on_device(
    patches,
    embed_weight,
    embed_bias,
    queries,
    score_bias,
    key_weight,
    value_weight,
    out_weight,
    out_bias,
):
    var_count = lax.axis_size("var")
    mp_count = lax.axis_size("mp")
    var_place = lax.axis_index("var")
    local_vars, tok_rows, _ = patches.shape
    all_vars = local_vars * var_count
    tile_width = embed_weight.shape[2]
    quarter = tile_width // var_count
    part_tokens = tok_rows // var_count
    rows = part_tokens * all_vars
    f32 = jnp.float32
    embedded = jnp.einsum("vtp,vpc->vtc", patches, embed_weight, preferred_element_type=f32)
    embedded = (embedded + embed_bias[:, None, :].astype(f32)).astype(jnp.bfloat16)
    own = embedded.reshape(local_vars, var_count, part_tokens, var_count, quarter)
    own = own.transpose(3, 1, 0, 2, 4).reshape(var_count, var_count, -1, quarter)
    order = arrival_order(np.arange(mp_count)[:, None])
    order = jnp.take(jnp.asarray(order, jnp.int32), lax.axis_index("mp"), axis=0)
    *weights, ordered = ordered_weights(order, key_weight, value_weight, (8, 8, 8, 4, 4))
    received = lax.all_to_all(own, "var", split_axis=0, concat_axis=0, tiled=True)
    groups = jnp.stack([(var_place + step) % var_count for step in STEPS]).astype(jnp.int32)
    weights = [w.reshape(-1, 2 * tile_width) for w in weights]
    early = pack(received, groups, 0, 2, ordered)
    late = pack(received, groups, 2, 2, early)
    early = [early] + [along_z(early, step) for step in (1, 3, 2)]
    late = [late] + [along_z(late, step) for step in (1, 3, 2)]
    early += [other_core(part) for part in early]

    def product(line, near, far):
        total = 0.0
        for part, weight in zip([line, near, other_core(near), far, other_core(far)], weights):
            total = total + jnp.dot(part, weight, preferred_element_type=f32)
        return total

    core = lax.axis_index("mp") % C
    line0 = line_of(early, 0, late[1], late[2])
    near0 = along_y(line0)
    line1 = line_of(early, 1, line0, line0)
    near1 = along_y(line1)
    half0 = first_half(near0, line1)
    far0 = along_y(half0)
    late += [other_core(part) for part in late]
    line2 = line_of(late, 0, half0, half0)
    near2 = along_y(line2)
    half1 = first_half(near1, line2)
    far1 = along_y(half1)
    line3 = line_of(late, 1, half1, half1)
    near3 = along_y(line3)
    far0 = copied(far0, line3)
    far_sent = product(line0, near0, far0).astype(jnp.bfloat16)
    far = core_var_shift(far_sent).astype(f32)
    half2 = first_half(near2, far_sent)
    far2 = along_y(half2)
    far1 = copied(far1, half2)
    half3 = first_half(near3, far1)
    far3 = along_y(half3)
    ahead_sent = product(line1, near1, far1) + jnp.where(core == 0, far, 0.0)
    ahead_sent = ahead_sent.astype(jnp.bfloat16)
    far2 = copied(far2, half3)
    behind_sent = product(line2, near2, far2) + jnp.where(core == 1, far, 0.0)
    behind_sent = behind_sent.astype(jnp.bfloat16)
    from_behind = var_shift(ahead_sent, 1)
    from_ahead = var_shift(behind_sent, -1)
    far3 = copied(far3, behind_sent)
    totals = product(line3, near3, far3)
    totals = totals + from_behind.astype(f32) + from_ahead.astype(f32)

    keys, values = totals[:, :tile_width], totals[:, tile_width:]
    scale = lax.rsqrt(jnp.mean(keys * keys, axis=1) + 1e-06)
    query_rows = lax.dynamic_slice_in_dim(queries, var_place * part_tokens, part_tokens, 0)
    bias_rows = lax.dynamic_slice_in_dim(score_bias, var_place * part_tokens, part_tokens, 0)
    token = np.arange(rows) % part_tokens
    spot = jnp.asarray(token[:, None] == np.arange(part_tokens))
    spread = jnp.dot(spot.astype(jnp.bfloat16), query_rows, preferred_element_type=f32)
    scores = (spread * keys).sum(1) * scale / math.sqrt(HD) + bias_rows.T.reshape(rows)
    scores = jnp.where(spot, scores[:, None], -jnp.inf)
    weight = jnp.exp(scores - scores.max(0, keepdims=True))
    attention = weight / weight.sum(0, keepdims=True)
    mixed = lax.dot_general(
        attention, values, (((0,), (0,)), ((), ())), precision=lax.Precision.HIGHEST
    ).astype(jnp.bfloat16)

    every_token = jnp.zeros((tok_rows, tile_width), jnp.bfloat16)
    for step in range(var_count):
        piece = var_shift(mixed, step) if step else mixed
        place = (var_place - step) % var_count
        every_token = lax.dynamic_update_slice_in_dim(every_token, piece, place * part_tokens, 0)
    product = jnp.dot(every_token, out_weight, preferred_element_type=f32)
    product = product.astype(jnp.bfloat16).reshape(tok_rows, mp_count, -1).transpose(1, 0, 2)
    terms = lax.all_to_all(product, "mp", split_axis=0, concat_axis=0, tiled=True)
    summed = terms.astype(f32).sum(0)
    return (summed + out_bias.astype(f32)[None, :]).astype(jnp.bfloat16)


def solution(mesh):
    in_specs = (
        P("var", "tok", None),
        P("var", None, "mp"),
        P("var", "mp"),
        P("tok", "mp"),
        P("tok", None),
        P(None, "var", "mp"),
        P(None, "var", "mp"),
        P("mp", "var"),
        P(("var", "mp")),
    )
    out_specs = P("tok", ("var", "mp"))
    return jax.shard_map(
        on_device, mesh=mesh, in_specs=in_specs, out_specs=out_specs, check_vma=False
    )
```

```python
import functools
import math

import jax
import jax.numpy as jnp
import numpy as np
from jax import lax
from jax.experimental import pallas as pl
from jax.experimental.pallas import tpu as pltpu
from jax.sharding import PartitionSpec as P

HD = 384
Z, Y, C = 4, 4, 2
STEPS = (2, 1, 3, 0)
COST = 2**16
VMEM = 8 * 2**20


def move(array, there):
    pairs = []
    for z in range(Z):
        for y in range(Y):
            for c in range(C):
                z2, y2, c2 = there(z, y, c)
                pairs.append(((z * Y + y) * C + c, ((z2 % Z) * Y + y2 % Y) * C + c2 % C))
    return lax.ppermute(array, "mp", pairs)


def other_core(array):
    return move(array, lambda z, y, c: (z, y, 1 - c))


def along_z(array, step):
    return move(array, lambda z, y, c: (z + step, y, c))


def along_y(array):
    return move(array, lambda z, y, c: (z, y + 1 - 2 * c, c))


def local_call(
    kernel, after, arrays, specs, out_shape, out_block, name, dtype=jnp.bfloat16
):
    return pl.pallas_call(
        kernel,
        grid=(1,),
        in_specs=[pl.BlockSpec(memory_space=pl.ANY)] + specs,
        out_specs=out_block,
        out_shape=jax.ShapeDtypeStruct(out_shape, dtype),
        compiler_params=pltpu.CompilerParams(vmem_limit_bytes=VMEM),
        cost_estimate=pl.CostEstimate(flops=0, transcendentals=0, bytes_accessed=COST),
        name=name,
    )(after, *arrays)


def copy_kernel(after, array, out):
    if len(out.shape) == 2 and out.shape[0] % 16 == 0:

        @pl.loop(0, out.shape[0] // 16)
        def _(n):
            rows = pl.ds(pl.multiple_of(n * 16, 16), 16)
            out[rows, :] = array[rows, :]

    else:
        out[...] = array[...]


def pack_kernel(first, groups, after, received, out):
    owners, width = received.shape[0], received.shape[3]

    @pl.loop(0, out.shape[0])
    def _(chunk):
        for owner in range(owners):
            out[chunk, :, owner * width : (owner + 1) * width] = received[
                owner, groups[first + chunk]
            ]


def pack(received, groups, first, count, after):
    owners, _, rows, width = received.shape
    return pl.pallas_call(
        functools.partial(pack_kernel, first),
        in_specs=[
            pl.BlockSpec(memory_space=pltpu.SMEM),
            pl.BlockSpec(memory_space=pl.ANY),
            pl.BlockSpec(memory_space=pltpu.VMEM),
        ],
        out_specs=pl.BlockSpec(memory_space=pltpu.VMEM),
        out_shape=jax.ShapeDtypeStruct((count, rows, owners * width), jnp.bfloat16),
        compiler_params=pltpu.CompilerParams(vmem_limit_bytes=VMEM),
        cost_estimate=pl.CostEstimate(flops=0, transcendentals=0, bytes_accessed=COST),
        name="pack",
    )(groups, after, received)


def first_half(array, after):
    rows, width = array.shape
    block = pl.BlockSpec((rows, width // 2), lambda k: (0, 0))
    return local_call(copy_kernel, after, [array], [block], (rows, width // 2), block, "half")


def line_kernel(chunk, first, second, *refs):
    *parts, out, wide = refs
    tile = out.shape[1] // len(parts)
    rows = parts[0].shape[1]
    for n, part in enumerate(parts):
        values = part[chunk].astype(jnp.float32)
        for block in range(values.shape[1] // tile):
            wide[block * rows : (block + 1) * rows, n * tile : (n + 1) * tile] = values[
                :, block * tile : (block + 1) * tile
            ]

    @pl.loop(0, out.shape[0] // 16)
    def _(n):
        group = pl.ds(pl.multiple_of(n * 16, 16), 16)
        out[group, :] = wide[group, :].astype(out.dtype)


def line_of(parts, chunk, *after):
    _, rows, width = parts[0].shape
    tile = width // 4
    shape = (rows * 4, tile * len(parts))
    return pl.pallas_call(
        functools.partial(line_kernel, chunk),
        in_specs=[pl.BlockSpec(memory_space=pl.ANY)] * 2
        + [pl.BlockSpec(memory_space=pltpu.VMEM) for _ in parts],
        out_specs=pl.BlockSpec(memory_space=pltpu.VMEM),
        out_shape=jax.ShapeDtypeStruct(shape, jnp.bfloat16),
        scratch_shapes=[pltpu.VMEM(shape, jnp.float32)],
        compiler_params=pltpu.CompilerParams(vmem_limit_bytes=VMEM),
        cost_estimate=pl.CostEstimate(flops=0, transcendentals=0, bytes_accessed=COST),
        name="line",
    )(*after, *parts)


def copied(array, after):
    block = pl.BlockSpec(array.shape, lambda k: (0,) * array.ndim)
    return local_call(
        copy_kernel, after, [array], [block], array.shape, block, "copied", array.dtype
    )


def order_kernel(order, keys, values, *refs):
    *outs, done, held, sems, out_sems = refs
    done[...] = jnp.zeros_like(done)
    width = keys.shape[2]

    def copies(n):
        return [
            pltpu.make_async_copy(
                weight.at[order[n]], held.at[n, :, pl.ds(k * width, width)], sems.at[k, n]
            )
            for k, weight in enumerate((keys, values))
        ]

    @pl.loop(0, keys.shape[0])
    def _(n):
        for copy in copies(n):
            copy.start()

    leaving = []
    first = 0
    for m, out in enumerate(outs):
        last = first + out.shape[0]

        @pl.loop(first, last)
        def _(n):
            for copy in copies(n):
                copy.wait()

        leaving.append(
            pltpu.make_async_copy(held.at[pl.ds(first, last - first)], out, out_sems.at[m])
        )
        leaving[-1].start()
        first = last
    for copy in leaving:
        copy.wait()


def ordered_weights(order, keys, values, counts):
    tiles, rows, width = keys.shape
    anywhere = pl.BlockSpec(memory_space=pl.ANY)
    return pl.pallas_call(
        order_kernel,
        in_specs=[pl.BlockSpec(memory_space=pltpu.SMEM), anywhere, anywhere],
        out_specs=[pl.BlockSpec(memory_space=pltpu.HBM) for _ in counts]
        + [pl.BlockSpec(memory_space=pltpu.VMEM)],
        out_shape=[pltpu.HBM((n, rows, 2 * width), keys.dtype) for n in counts]
        + [jax.ShapeDtypeStruct((8, 128), jnp.float32)],
        scratch_shapes=[
            pltpu.VMEM((tiles, rows, 2 * width), keys.dtype),
            pltpu.SemaphoreType.DMA((2, tiles)),
            pltpu.SemaphoreType.DMA((len(counts),)),
        ],
        compiler_params=pltpu.CompilerParams(vmem_limit_bytes=VMEM),
        cost_estimate=pl.CostEstimate(flops=0, transcendentals=0, bytes_accessed=10 * 2**20),
        name="order_weights",
    )(order, keys, values)


def arrival_order(ids):
    def sent(ids, there):
        result = np.zeros_like(ids)
        for n in range(Z * Y * C):
            z, y, c = there(n // (Y * C), n // C % Y, n % C)
            result[(z % Z * Y + y % Y) * C + c % C] = ids[n]
        return result

    def up_or_down(ids):
        return sent(ids, lambda z, y, c: (z, y + 1 - 2 * c, c))

    def swapped(ids):
        return sent(ids, lambda z, y, c: (z, y, 1 - c))

    mine = [ids] + [sent(ids, lambda z, y, c: (z + step, y, c)) for step in (1, 3, 2)]
    line = np.concatenate(mine + [swapped(part) for part in mine], axis=1)
    near = up_or_down(line)
    far = up_or_down(near[:, : near.shape[1] // 2])
    return np.concatenate([line, near, swapped(near), far, swapped(far)], axis=1)


def core_var_shift(array):
    n = lax.axis_size("var")
    m = lax.axis_size("mp")
    pairs = [
        (k * m + p, (k + 1 - 2 * (p % C)) % n * m + p) for k in range(n) for p in range(m)
    ]
    return lax.ppermute(array, ("var", "mp"), pairs)


def var_shift(array, step):
    n = lax.axis_size("var")
    return lax.ppermute(array, "var", [(k, (k + step) % n) for k in range(n)])


def on_device(
    patches,
    embed_weight,
    embed_bias,
    queries,
    score_bias,
    key_weight,
    value_weight,
    out_weight,
    out_bias,
):
    var_count = lax.axis_size("var")
    mp_count = lax.axis_size("mp")
    var_place = lax.axis_index("var")
    local_vars, tok_rows, _ = patches.shape
    all_vars = local_vars * var_count
    tile_width = embed_weight.shape[2]
    quarter = tile_width // var_count
    part_tokens = tok_rows // var_count
    rows = part_tokens * all_vars
    f32 = jnp.float32
    embedded = jnp.einsum("vtp,vpc->vtc", patches, embed_weight, preferred_element_type=f32)
    embedded = (embedded + embed_bias[:, None, :].astype(f32)).astype(jnp.bfloat16)
    own = embedded.reshape(local_vars, var_count, part_tokens, var_count, quarter)
    own = own.transpose(3, 1, 0, 2, 4).reshape(var_count, var_count, -1, quarter)
    order = arrival_order(np.arange(mp_count)[:, None])
    order = jnp.take(jnp.asarray(order, jnp.int32), lax.axis_index("mp"), axis=0)
    *weights, ordered = ordered_weights(order, key_weight, value_weight, (8, 8, 8, 4, 4))
    received = lax.all_to_all(own, "var", split_axis=0, concat_axis=0, tiled=True)
    groups = jnp.stack([(var_place + step) % var_count for step in STEPS]).astype(jnp.int32)
    weights = [w.reshape(-1, 2 * tile_width) for w in weights]
    early = pack(received, groups, 0, 2, ordered)
    late = pack(received, groups, 2, 2, early)
    early = [early] + [along_z(early, step) for step in (1, 3, 2)]
    late = [late] + [along_z(late, step) for step in (1, 3, 2)]
    early += [other_core(part) for part in early]

    def product(line, near, far):
        total = 0.0
        for part, weight in zip([line, near, other_core(near), far, other_core(far)], weights):
            total = total + jnp.dot(part, weight, preferred_element_type=f32)
        return total

    core = lax.axis_index("mp") % C
    line0 = line_of(early, 0, late[1], late[2])
    near0 = along_y(line0)
    line1 = line_of(early, 1, line0, line0)
    near1 = along_y(line1)
    half0 = first_half(near0, line1)
    far0 = along_y(half0)
    late[3] = copied(late[3], half0)
    late += [other_core(part) for part in late]
    half1 = first_half(near1, half0)
    far1 = along_y(half1)
    line2 = line_of(late, 0, half1, half1)
    near2 = along_y(line2)
    far0 = copied(far0, line2)
    far_sent = product(line0, near0, far0).astype(jnp.bfloat16)
    far = core_var_shift(far_sent).astype(f32)
    half2 = first_half(near2, far_sent)
    far2 = along_y(half2)
    line3 = line_of(late, 1, half2, half2)
    near3 = along_y(line3)
    far1 = copied(far1, line3)
    ahead_sent = product(line1, near1, far1) + jnp.where(core == 0, far, 0.0)
    ahead_sent = ahead_sent.astype(jnp.bfloat16)
    far2 = copied(far2, far1)
    behind_sent = product(line2, near2, far2) + jnp.where(core == 1, far, 0.0)
    behind_sent = behind_sent.astype(jnp.bfloat16)
    from_behind = var_shift(ahead_sent, 1)
    from_ahead = var_shift(behind_sent, -1)
    half3 = first_half(near3, behind_sent)
    far3 = along_y(half3)
    totals = product(line3, near3, far3)
    totals = totals + from_behind.astype(f32) + from_ahead.astype(f32)

    keys, values = totals[:, :tile_width], totals[:, tile_width:]
    scale = lax.rsqrt(jnp.mean(keys * keys, axis=1) + 1e-06)
    query_rows = lax.dynamic_slice_in_dim(
        copied(queries, behind_sent), var_place * part_tokens, part_tokens, 0)
    bias_rows = lax.dynamic_slice_in_dim(
        copied(score_bias, behind_sent), var_place * part_tokens, part_tokens, 0)
    token = np.arange(rows) % part_tokens
    spot = jnp.asarray(token[:, None] == np.arange(part_tokens))
    spread = jnp.dot(spot.astype(jnp.bfloat16), query_rows, preferred_element_type=f32)
    spread = lax.optimization_barrier(spread)
    scores = (spread * keys).sum(1) * scale / math.sqrt(HD) + bias_rows.T.reshape(rows)
    scores = jnp.where(spot, scores[:, None], -jnp.inf)
    weight = jnp.exp(scores - scores.max(0, keepdims=True))
    attention = weight / weight.sum(0, keepdims=True)
    mixed = lax.dot_general(
        attention, values, (((0,), (0,)), ((), ())), precision=lax.Precision.HIGHEST
    ).astype(jnp.bfloat16)

    every_token = jnp.zeros((tok_rows, tile_width), jnp.bfloat16)
    for step in (2, 1, 3, 0):
        piece = var_shift(mixed, step) if step else mixed
        place = (var_place - step) % var_count
        every_token = lax.dynamic_update_slice_in_dim(every_token, piece, place * part_tokens, 0)
    product = jnp.dot(every_token, out_weight, preferred_element_type=f32)
    product = product.astype(jnp.bfloat16).reshape(tok_rows, mp_count, -1).transpose(1, 0, 2)
    terms = lax.all_to_all(product, "mp", split_axis=0, concat_axis=0, tiled=True)
    summed = terms.astype(f32).sum(0)
    return (summed + out_bias.astype(f32)[None, :]).astype(jnp.bfloat16)


def solution(mesh):
    in_specs = (
        P("var", "tok", None),
        P("var", None, "mp"),
        P("var", "mp"),
        P("tok", "mp"),
        P("tok", None),
        P(None, "var", "mp"),
        P(None, "var", "mp"),
        P("mp", "var"),
        P(("var", "mp")),
    )
    out_specs = P("tok", ("var", "mp"))
    return jax.shard_map(
        on_device, mesh=mesh, in_specs=in_specs, out_specs=out_specs, check_vma=False
    )
```

```python
import functools
import math

import jax
import jax.numpy as jnp
import numpy as np
from jax import lax
from jax.experimental import pallas as pl
from jax.experimental.pallas import tpu as pltpu
from jax.sharding import PartitionSpec as P

HD = 384
Z, Y, C = 4, 4, 2
STEPS = (2, 1, 3, 0)
COST = 2**16
VMEM = 8 * 2**20


def move(array, there):
    pairs = []
    for z in range(Z):
        for y in range(Y):
            for c in range(C):
                z2, y2, c2 = there(z, y, c)
                pairs.append(((z * Y + y) * C + c, ((z2 % Z) * Y + y2 % Y) * C + c2 % C))
    return lax.ppermute(array, "mp", pairs)


def other_core(array):
    return move(array, lambda z, y, c: (z, y, 1 - c))


def along_z(array, step):
    return move(array, lambda z, y, c: (z + step, y, c))


def along_y(array):
    return move(array, lambda z, y, c: (z, y + 1 - 2 * c, c))


def local_call(
    kernel, after, arrays, specs, out_shape, out_block, name, dtype=jnp.bfloat16
):
    return pl.pallas_call(
        kernel,
        grid=(1,),
        in_specs=[pl.BlockSpec(memory_space=pl.ANY)] + specs,
        out_specs=out_block,
        out_shape=jax.ShapeDtypeStruct(out_shape, dtype),
        compiler_params=pltpu.CompilerParams(vmem_limit_bytes=VMEM),
        cost_estimate=pl.CostEstimate(flops=0, transcendentals=0, bytes_accessed=COST),
        name=name,
    )(after, *arrays)


def copy_kernel(after, array, out):
    if len(out.shape) == 2 and out.shape[0] % 16 == 0:

        @pl.loop(0, out.shape[0] // 16)
        def _(n):
            rows = pl.ds(pl.multiple_of(n * 16, 16), 16)
            out[rows, :] = array[rows, :]

    else:
        out[...] = array[...]


def pack_kernel(first, groups, after, received, out):
    owners, width = received.shape[0], received.shape[3]

    @pl.loop(0, out.shape[0])
    def _(chunk):
        for owner in range(owners):
            out[chunk, :, owner * width : (owner + 1) * width] = received[
                owner, groups[first + chunk]
            ]


def pack(received, groups, first, count, after):
    owners, _, rows, width = received.shape
    return pl.pallas_call(
        functools.partial(pack_kernel, first),
        in_specs=[
            pl.BlockSpec(memory_space=pltpu.SMEM),
            pl.BlockSpec(memory_space=pl.ANY),
            pl.BlockSpec(memory_space=pltpu.VMEM),
        ],
        out_specs=pl.BlockSpec(memory_space=pltpu.VMEM),
        out_shape=jax.ShapeDtypeStruct((count, rows, owners * width), jnp.bfloat16),
        compiler_params=pltpu.CompilerParams(vmem_limit_bytes=VMEM),
        cost_estimate=pl.CostEstimate(flops=0, transcendentals=0, bytes_accessed=COST),
        name="pack",
    )(groups, after, received)


def first_half(array, after):
    rows, width = array.shape
    block = pl.BlockSpec((rows, width // 2), lambda k: (0, 0))
    return local_call(copy_kernel, after, [array], [block], (rows, width // 2), block, "half")


def line_kernel(chunk, first, second, *refs):
    *parts, out, wide = refs
    tile = out.shape[1] // len(parts)
    rows = parts[0].shape[1]
    for n, part in enumerate(parts):
        values = part[chunk].astype(jnp.float32)
        for block in range(values.shape[1] // tile):
            wide[block * rows : (block + 1) * rows, n * tile : (n + 1) * tile] = values[
                :, block * tile : (block + 1) * tile
            ]

    @pl.loop(0, out.shape[0] // 16)
    def _(n):
        group = pl.ds(pl.multiple_of(n * 16, 16), 16)
        out[group, :] = wide[group, :].astype(out.dtype)


def line_of(parts, chunk, *after):
    _, rows, width = parts[0].shape
    tile = width // 4
    shape = (rows * 4, tile * len(parts))
    return pl.pallas_call(
        functools.partial(line_kernel, chunk),
        in_specs=[pl.BlockSpec(memory_space=pl.ANY)] * 2
        + [pl.BlockSpec(memory_space=pltpu.VMEM) for _ in parts],
        out_specs=pl.BlockSpec(memory_space=pltpu.VMEM),
        out_shape=jax.ShapeDtypeStruct(shape, jnp.bfloat16),
        scratch_shapes=[pltpu.VMEM(shape, jnp.float32)],
        compiler_params=pltpu.CompilerParams(vmem_limit_bytes=VMEM),
        cost_estimate=pl.CostEstimate(flops=0, transcendentals=0, bytes_accessed=COST),
        name="line",
    )(*after, *parts)


def copied(array, after):
    block = pl.BlockSpec(array.shape, lambda k: (0,) * array.ndim)
    return local_call(
        copy_kernel, after, [array], [block], array.shape, block, "copied", array.dtype
    )


def order_kernel(order, keys, values, *refs):
    *outs, done, held, sems, out_sems = refs
    done[...] = jnp.zeros_like(done)
    width = keys.shape[2]

    def copies(n):
        return [
            pltpu.make_async_copy(
                weight.at[order[n]], held.at[n, :, pl.ds(k * width, width)], sems.at[k, n]
            )
            for k, weight in enumerate((keys, values))
        ]

    @pl.loop(0, keys.shape[0])
    def _(n):
        for copy in copies(n):
            copy.start()

    leaving = []
    first = 0
    for m, out in enumerate(outs):
        last = first + out.shape[0]

        @pl.loop(first, last)
        def _(n):
            for copy in copies(n):
                copy.wait()

        leaving.append(
            pltpu.make_async_copy(held.at[pl.ds(first, last - first)], out, out_sems.at[m])
        )
        leaving[-1].start()
        first = last
    for copy in leaving:
        copy.wait()


def ordered_weights(order, keys, values, counts):
    tiles, rows, width = keys.shape
    anywhere = pl.BlockSpec(memory_space=pl.ANY)
    return pl.pallas_call(
        order_kernel,
        in_specs=[pl.BlockSpec(memory_space=pltpu.SMEM), anywhere, anywhere],
        out_specs=[pl.BlockSpec(memory_space=pltpu.HBM) for _ in counts]
        + [pl.BlockSpec(memory_space=pltpu.VMEM)],
        out_shape=[pltpu.HBM((n, rows, 2 * width), keys.dtype) for n in counts]
        + [jax.ShapeDtypeStruct((8, 128), jnp.float32)],
        scratch_shapes=[
            pltpu.VMEM((tiles, rows, 2 * width), keys.dtype),
            pltpu.SemaphoreType.DMA((2, tiles)),
            pltpu.SemaphoreType.DMA((len(counts),)),
        ],
        compiler_params=pltpu.CompilerParams(vmem_limit_bytes=VMEM),
        cost_estimate=pl.CostEstimate(flops=0, transcendentals=0, bytes_accessed=10 * 2**20),
        name="order_weights",
    )(order, keys, values)


def arrival_order(ids):
    def sent(ids, there):
        result = np.zeros_like(ids)
        for n in range(Z * Y * C):
            z, y, c = there(n // (Y * C), n // C % Y, n % C)
            result[(z % Z * Y + y % Y) * C + c % C] = ids[n]
        return result

    def up_or_down(ids):
        return sent(ids, lambda z, y, c: (z, y + 1 - 2 * c, c))

    def swapped(ids):
        return sent(ids, lambda z, y, c: (z, y, 1 - c))

    mine = [ids] + [sent(ids, lambda z, y, c: (z + step, y, c)) for step in (1, 3, 2)]
    line = np.concatenate(mine + [swapped(part) for part in mine], axis=1)
    near = up_or_down(line)
    far = up_or_down(near[:, : near.shape[1] // 2])
    return np.concatenate([line, near, swapped(near), far, swapped(far)], axis=1)


def core_var_shift(array):
    n = lax.axis_size("var")
    m = lax.axis_size("mp")
    pairs = [
        (k * m + p, (k + 1 - 2 * (p % C)) % n * m + p) for k in range(n) for p in range(m)
    ]
    return lax.ppermute(array, ("var", "mp"), pairs)


def var_shift(array, step):
    n = lax.axis_size("var")
    return lax.ppermute(array, "var", [(k, (k + step) % n) for k in range(n)])


def on_device(
    patches,
    embed_weight,
    embed_bias,
    queries,
    score_bias,
    key_weight,
    value_weight,
    out_weight,
    out_bias,
):
    var_count = lax.axis_size("var")
    mp_count = lax.axis_size("mp")
    var_place = lax.axis_index("var")
    local_vars, tok_rows, _ = patches.shape
    all_vars = local_vars * var_count
    tile_width = embed_weight.shape[2]
    quarter = tile_width // var_count
    part_tokens = tok_rows // var_count
    rows = part_tokens * all_vars
    f32 = jnp.float32
    embedded = jnp.einsum("vtp,vpc->vtc", patches, embed_weight, preferred_element_type=f32)
    embedded = (embedded + embed_bias[:, None, :].astype(f32)).astype(jnp.bfloat16)
    own = embedded.reshape(local_vars, var_count, part_tokens, var_count, quarter)
    own = own.transpose(3, 1, 0, 2, 4).reshape(var_count, var_count, -1, quarter)
    order = arrival_order(np.arange(mp_count)[:, None])
    order = jnp.take(jnp.asarray(order, jnp.int32), lax.axis_index("mp"), axis=0)
    *weights, ordered = ordered_weights(order, key_weight, value_weight, (8, 8, 8, 4, 4))
    received = lax.all_to_all(own, "var", split_axis=0, concat_axis=0, tiled=True)
    groups = jnp.stack([(var_place + step) % var_count for step in STEPS]).astype(jnp.int32)
    weights = [w.reshape(-1, 2 * tile_width) for w in weights]
    early = pack(received, groups, 0, 2, out_bias)
    late = pack(received, groups, 2, 2, early)
    early = [early] + [along_z(early, step) for step in (1, 3, 2)]
    late = [late] + [along_z(late, step) for step in (1, 3, 2)]
    early += [other_core(copied(early[0], ordered))] + [other_core(part) for part in early[1:]]

    def product(line, near, far):
        total = 0.0
        for part, weight in zip([line, near, other_core(near), far, other_core(far)], weights):
            total = total + jnp.dot(part, weight, preferred_element_type=f32)
        return total

    core = lax.axis_index("mp") % C
    line0 = line_of(early, 0, late[1], late[2])
    near0 = along_y(line0)
    line1 = line_of(early, 1, line0, line0)
    near1 = along_y(line1)
    half0 = first_half(near0, line1)
    far0 = along_y(half0)
    late[3] = copied(late[3], half0)
    late += [other_core(part) for part in late]
    half1 = first_half(near1, half0)
    far1 = along_y(half1)
    line2 = line_of(late, 0, half1, half1)
    near2 = along_y(line2)
    far0 = copied(far0, line2)
    far_sent = product(line0, near0, far0).astype(jnp.bfloat16)
    far = core_var_shift(far_sent).astype(f32)
    half2 = first_half(near2, far_sent)
    far2 = along_y(half2)
    line3 = line_of(late, 1, half2, half2)
    near3 = along_y(line3)
    far1 = copied(far1, line3)
    ahead_sent = product(line1, near1, far1) + jnp.where(core == 0, far, 0.0)
    ahead_sent = ahead_sent.astype(jnp.bfloat16)
    far2 = copied(far2, far1)
    behind_sent = product(line2, near2, far2) + jnp.where(core == 1, far, 0.0)
    behind_sent = behind_sent.astype(jnp.bfloat16)
    from_behind = var_shift(ahead_sent, 1)
    from_ahead = var_shift(behind_sent, -1)
    half3 = first_half(near3, behind_sent)
    far3 = along_y(half3)
    totals = product(line3, near3, far3)
    totals = totals + from_behind.astype(f32) + from_ahead.astype(f32)

    keys, values = totals[:, :tile_width], totals[:, tile_width:]
    scale = lax.rsqrt(jnp.mean(keys * keys, axis=1) + 1e-06)
    query_rows = lax.dynamic_slice_in_dim(
        copied(queries, behind_sent), var_place * part_tokens, part_tokens, 0)
    bias_rows = lax.dynamic_slice_in_dim(
        copied(score_bias, behind_sent), var_place * part_tokens, part_tokens, 0)
    token = np.arange(rows) % part_tokens
    spot = jnp.asarray(token[:, None] == np.arange(part_tokens))
    spread = jnp.dot(spot.astype(jnp.bfloat16), query_rows, preferred_element_type=f32)
    spread = lax.optimization_barrier(spread)
    scores = (spread * keys).sum(1) * scale / math.sqrt(HD) + bias_rows.T.reshape(rows)
    scores = jnp.where(spot, scores[:, None], -jnp.inf)
    weight = jnp.exp(scores - scores.max(0, keepdims=True))
    attention = weight / weight.sum(0, keepdims=True)
    mixed = lax.dot_general(
        attention, values, (((0,), (0,)), ((), ())), precision=lax.Precision.HIGHEST
    ).astype(jnp.bfloat16)

    every_token = jnp.zeros((tok_rows, tile_width), jnp.bfloat16)
    for step in (2, 1, 3, 0):
        piece = var_shift(mixed, step) if step else mixed
        place = (var_place - step) % var_count
        every_token = lax.dynamic_update_slice_in_dim(every_token, piece, place * part_tokens, 0)
    product = jnp.dot(every_token, out_weight, preferred_element_type=f32)
    product = product.astype(jnp.bfloat16).reshape(tok_rows, mp_count, -1).transpose(1, 0, 2)
    terms = lax.all_to_all(product, "mp", split_axis=0, concat_axis=0, tiled=True)
    summed = terms.astype(f32).sum(0)
    return (summed + out_bias.astype(f32)[None, :]).astype(jnp.bfloat16)


def solution(mesh):
    in_specs = (
        P("var", "tok", None),
        P("var", None, "mp"),
        P("var", "mp"),
        P("tok", "mp"),
        P("tok", None),
        P(None, "var", "mp"),
        P(None, "var", "mp"),
        P("mp", "var"),
        P(("var", "mp")),
    )
    out_specs = P("tok", ("var", "mp"))
    return jax.shard_map(
        on_device, mesh=mesh, in_specs=in_specs, out_specs=out_specs, check_vma=False
    )
```
